32 devices in a mesh: grp: 2 (over y), mom: 4 (over z), orb: 2 (over x), ff: 2 (over core).
Axes of the slice: x: 2, y: 2, z: 4, core: 2. Of those that a mesh axis runs over, the one named last changes fastest.
Arguments:
- vertex_own: bfloat16 [64, 468, 468], P(('grp', 'mom'), 'orb', 'ff'), parts along dimension 0, may hold values from -6 to 6
- vertex_cross: bfloat16 [64, 468, 468], P(('grp', 'mom'), 'orb', 'ff'), parts along dimension 0, may hold values from -6 to 6
- project_coeff: bfloat16 [32, 32, 13, 13], P('mom'), may hold values from -0.3125 to 0.3125
- green_left: float32 [72, 2304], P('grp'), parts along dimension 0, may hold values from -6 to 6
- green_right: float32 [72, 2304], P('grp'), parts along dimension 0, may hold values from -0.30769232 to 0.30769232
- window: int32 [32], replicated, may hold values from 0 to 2303, as said below
- shifts: int32 [13, 2], replicated, may hold values from -3 to 3, as said below
Outputs:
- new_vertex: bfloat16 [64, 468, 468], P(('grp', 'mom'), 'orb', 'ff'), parts along dimension 0
The draws below stay inside these ranges and needn't reach their ends.
There are 2 independent parts, one for each index of `grp`. The reference program is written for one: setup_inputs(seed, part) draws one part's arguments, and reference() takes and returns one part's arrays. A program takes and returns all parts, laid end to end along the dimension named above; an argument that names none is the same for every part. Nothing has to cross between parts.
Inputs may be any that keep to these rules, and one draw needn't show every extreme that they name: `window`: 32 distinct lattice indices kx * 48 + ky. `shifts`: 13 distinct vectors (x, y) with x > 0, or x = 0 and y >= 0.
All inputs are finite; a program needn't handle non-finite values.
Results may differ from the reference program's by a relative error of at most 0.0066.
Values may be sent and summed in bfloat16 or wider, within the bound.
A program may use at most 128 MiB of HBM per device.

```python
import math
import jax
import jax.numpy as jnp
import numpy as np
from jax import lax

NF = 13
LX = 48
NP = 36
M = 468
NK = 2304
QT = 32


def draw_window(key, part):
    key = jax.random.fold_in(key, 11)
    return jax.random.permutation(key, NK)[:QT].astype(jnp.int32)


def draw_shifts(key, part):
    key = jax.random.fold_in(key, 23)
    candidates = np.array([[0, 0], [0, 1], [0, 2], [0, 3]] + [[x, y] for x in range(1, 4) for y in range(-3, 4)], dtype=np.int32)
    order = jax.random.permutation(key, candidates.shape[0])[:NF]
    return jnp.asarray(candidates)[order].astype(jnp.int32)


def steps_of(own_key, extent, split, least, largest):
    def one(dim, parts):
        draws = jax.random.uniform(jax.random.fold_in(jax.random.fold_in(own_key, 6), dim), (parts,), jnp.float32, least / len(split), largest / len(split))
        return jnp.repeat(jnp.exp(draws), extent[dim] // parts).reshape((-1,) + (1,) * (len(extent) - dim - 1))

    loudness = one(*split[0])
    for cut in split[1:]:
        loudness = loudness * one(*cut)
    return loudness


def scatter_about(rng, dims, spread, limit, pieces=(), kind=jnp.bfloat16):
    drawn = jax.random.normal(rng, dims, jnp.float32) * spread
    if len(pieces) > 0:
        drawn = steps_of(rng, dims, pieces, -0.22, 0.18) * drawn
    return jnp.clip(drawn, min=-limit, max=limit).astype(kind)


def setup_inputs(seed: int = 0, part: int = 0) -> dict:
    splits = jax.random.split(jax.random.key(seed), 8)
    part_keys = jax.random.split(jax.random.fold_in(splits[7], part), 8)
    vertex_own = scatter_about(part_keys[0], (QT, M, M), 1.0, 6.0, ((0, 4), (1, 2), (2, 2)))
    vertex_cross = scatter_about(part_keys[1], (QT, M, M), 1.0, 6.0, ((0, 4), (1, 2), (2, 2)))
    project_coeff = scatter_about(splits[2], (QT, QT, NF, NF), (QT * NF) ** -0.5, 0.3125, ((0, 4),))
    green_left = scatter_about(part_keys[3], (NP, NK), 1.0, 6.0, (), jnp.float32)
    green_right = scatter_about(part_keys[4], (NP, NK), (0.5 * LX / (NP * NF)), 0.30769232, (), jnp.float32)
    window = draw_window(jax.random.fold_in(splits[7], 71), part)
    shifts = draw_shifts(jax.random.fold_in(splits[7], 71), part)
    return dict(vertex_own=vertex_own, vertex_cross=vertex_cross, project_coeff=project_coeff, green_left=green_left, green_right=green_right, window=window, shifts=shifts)


def form_factors(shifts, momenta):
    row_x = momenta // LX
    row_y = momenta % LX
    turn_count = (shifts[:, 0:1] * row_x[None, :] + shifts[:, 1:2] * row_y[None, :]) % LX
    phases = turn_count.astype(jnp.float32) * (2.0 * math.pi / LX)
    anchor = (shifts[:, 0] == 0) & (shifts[:, 1] == 0)
    weight = jnp.where(anchor, 1.0, math.sqrt(2.0)).astype(jnp.float32)
    return weight[:, None] * jnp.cos(phases)

def folded(momenta, qpoint):
    row_x = (momenta // LX + qpoint // LX) % LX
    row_y = (momenta % LX + qpoint % LX) % LX
    return (row_x * LX + row_y).astype(jnp.int32)

def loop_left(green_left, form_table):
    loop_rows = green_left[:, None, :] * form_table[None, :, :]
    return loop_rows.reshape(-1, form_table.shape[1]).astype(jnp.bfloat16)

def loop_right(green_right, form_table, momenta, qpoint, total_count):
    picked = jnp.take(green_right, folded(momenta, qpoint), axis=1)
    loop_rows = picked[:, None, :] * form_table[None, :, :] * (1.0 / total_count)
    return loop_rows.reshape(-1, momenta.shape[0]).astype(jnp.bfloat16)

def reference(vertex_own, vertex_cross, project_coeff, green_left, green_right, window, shifts):
    momenta = jnp.arange(NK, dtype=jnp.int32)
    form_table = form_factors(shifts, momenta)
    left_loop = loop_left(green_left, form_table)
    stacked = vertex_cross.reshape(QT, NP, NF, M).transpose(0, 2, 1, 3).reshape(QT * NF, NP * M)

    def per_point(position):
        coeff_block = project_coeff[position].transpose(1, 0, 2).reshape(NF, QT * NF)
        projected = jnp.dot(coeff_block, stacked, preferred_element_type=jnp.float32)
        projected = projected.reshape(NF, NP, M).transpose(1, 0, 2).reshape(M, M)
        merged = (vertex_own[position].astype(jnp.float32) + projected).astype(jnp.bfloat16)
        right_loop = loop_right(green_right, form_table, momenta, window[position], NK)
        carried = jnp.dot(merged, left_loop, preferred_element_type=jnp.float32).astype(jnp.bfloat16)
        returned = jnp.dot(right_loop.T, merged, preferred_element_type=jnp.float32).astype(jnp.bfloat16)
        change = jnp.dot(carried, returned, preferred_element_type=jnp.float32)
        return (merged.astype(jnp.float32) + change).astype(jnp.bfloat16)
    return lax.map(per_point, jnp.arange(QT, dtype=jnp.int32))
```

```python
import math

import jax
import jax.numpy as jnp
from jax import lax
from jax.sharding import PartitionSpec as P

LX = 48


def form_factors(shifts, momenta):
    row_x = momenta // LX
    row_y = momenta % LX
    turn_count = (shifts[:, 0:1] * row_x[None, :] + shifts[:, 1:2] * row_y[None, :]) % LX
    phases = turn_count.astype(jnp.float32) * (2.0 * math.pi / LX)
    anchor = (shifts[:, 0] == 0) & (shifts[:, 1] == 0)
    weight = jnp.where(anchor, 1.0, math.sqrt(2.0)).astype(jnp.float32)
    return weight[:, None] * jnp.cos(phases)


def loop_left(green_part, form_table):
    loop_rows = green_part[:, None, :] * form_table[None, :, :]
    return loop_rows.reshape(-1, form_table.shape[1]).astype(jnp.bfloat16)


def shifted(doubled, momenta, qpoint, total_count):
    pairs = doubled.shape[0]
    step_y = qpoint % LX
    straight = lax.dynamic_slice(doubled, (0, qpoint), (pairs, total_count))
    back = (qpoint - LX + total_count) % total_count
    wrapped = lax.dynamic_slice(doubled, (0, back), (pairs, total_count))
    return jnp.where(momenta[None, :] % LX + step_y < LX, straight, wrapped)


def loop_right_all(green_right, form_table, momenta, qpoints, total_count):
    doubled = jnp.concatenate([green_right, green_right], axis=1)
    picked = jnp.stack(
        [shifted(doubled, momenta, qpoints[i], total_count) for i in range(qpoints.shape[0])]
    )
    loop_rows = picked[:, :, None, :] * form_table[None, None, :, :] * (1.0 / total_count)
    return loop_rows.reshape(qpoints.shape[0], -1, momenta.shape[0]).astype(jnp.bfloat16)


def body(vertex_own, vertex_cross, project_coeff, green_left, green_right, window, shifts):
    points, row_count, col_count = vertex_own.shape
    form_count = shifts.shape[0]
    pair_rows = row_count // form_count
    total_k = green_left.shape[1]
    my_start = lax.axis_index("mom") * points
    my_window = lax.dynamic_slice_in_dim(window, my_start, points, 0)
    arrived = lax.all_gather(vertex_cross, "mom", axis=0, tiled=True)
    momenta = jnp.arange(total_k, dtype=jnp.int32)
    form_table = form_factors(shifts, momenta)
    left_loop = loop_left(green_left, form_table)
    right_loop = loop_right_all(green_right, form_table, momenta, my_window, total_k)
    bubble = jnp.einsum(
        "jk,qik->qji", left_loop, right_loop, preferred_element_type=jnp.float32
    ).astype(jnp.bfloat16)
    count = arrived.shape[0]
    tiles = arrived.reshape(count, pair_rows, form_count, col_count)
    projected = jnp.einsum(
        "qplm,pamc->qalc", project_coeff, tiles, preferred_element_type=jnp.float32
    )
    merged = (
        vertex_own.astype(jnp.float32) + projected.reshape(points, row_count, col_count)
    ).astype(jnp.bfloat16)
    tall_block = lax.all_gather(merged, "orb", axis=1, tiled=True)
    wide_block = lax.all_gather(merged, "ff", axis=2, tiled=True)
    half = jnp.einsum(
        "qrj,qji->qri", wide_block, bubble, preferred_element_type=jnp.float32
    ).astype(jnp.bfloat16)
    change = jnp.einsum("qri,qic->qrc", half, tall_block, preferred_element_type=jnp.float32)
    return (merged.astype(jnp.float32) + change).astype(jnp.bfloat16)


def solution(mesh):
    return jax.shard_map(
        body,
        mesh=mesh,
        in_specs=(
            P(("grp", "mom"), "orb", "ff"),
            P(("grp", "mom"), "orb", "ff"),
            P("mom", None, None, None),
            P("grp", None),
            P("grp", None),
            P(),
            P(),
        ),
        out_specs=P(("grp", "mom"), "orb", "ff"),
        check_vma=False,
    )
```

```python
import math

import jax
import jax.numpy as jnp
from jax import lax
from jax.sharding import PartitionSpec as P

LX = 48


def form_factors(shifts, momenta):
    row_x = momenta // LX
    row_y = momenta % LX
    turn_count = (shifts[:, 0:1] * row_x[None, :] + shifts[:, 1:2] * row_y[None, :]) % LX
    phases = turn_count.astype(jnp.float32) * (2.0 * math.pi / LX)
    anchor = (shifts[:, 0] == 0) & (shifts[:, 1] == 0)
    weight = jnp.where(anchor, 1.0, math.sqrt(2.0)).astype(jnp.float32)
    return weight[:, None] * jnp.cos(phases)


def loop_left(green_part, form_table):
    loop_rows = green_part[:, None, :] * form_table[None, :, :]
    return loop_rows.reshape(-1, form_table.shape[1]).astype(jnp.bfloat16)


def shifted(doubled, momenta, qpoint, total_count):
    pairs = doubled.shape[0]
    step_y = qpoint % LX
    straight = lax.dynamic_slice(doubled, (0, qpoint), (pairs, total_count))
    back = (qpoint - LX + total_count) % total_count
    wrapped = lax.dynamic_slice(doubled, (0, back), (pairs, total_count))
    return jnp.where(momenta[None, :] % LX + step_y < LX, straight, wrapped)


def loop_right_all(green_right, form_table, momenta, qpoints, total_count):
    doubled = jnp.concatenate([green_right, green_right], axis=1)
    picked = jnp.stack(
        [shifted(doubled, momenta, qpoints[i], total_count) for i in range(qpoints.shape[0])]
    )
    loop_rows = picked[:, :, None, :] * form_table[None, None, :, :] * (1.0 / total_count)
    return loop_rows.reshape(qpoints.shape[0], -1, momenta.shape[0]).astype(jnp.bfloat16)


def body_gathered(vertex_own, vertex_cross, project_coeff, green_left, green_right, window, shifts):
    points, row_count, col_count = vertex_own.shape
    form_count = shifts.shape[0]
    pair_rows = row_count // form_count
    total_k = green_left.shape[1]
    my_start = lax.axis_index("mom") * points
    my_window = lax.dynamic_slice_in_dim(window, my_start, points, 0)
    arrived = lax.all_gather(vertex_cross, "mom", axis=0, tiled=True)
    momenta = jnp.arange(total_k, dtype=jnp.int32)
    form_table = form_factors(shifts, momenta)
    left_loop = loop_left(green_left, form_table)
    right_loop = loop_right_all(green_right, form_table, momenta, my_window, total_k)
    bubble = jnp.einsum(
        "jk,qik->qji", left_loop, right_loop, preferred_element_type=jnp.float32
    ).astype(jnp.bfloat16)
    count = arrived.shape[0]
    tiles = arrived.reshape(count, pair_rows, form_count, col_count)
    projected = jnp.einsum(
        "qplm,pamc->qalc", project_coeff, tiles, preferred_element_type=jnp.float32
    )
    merged = (
        vertex_own.astype(jnp.float32) + projected.reshape(points, row_count, col_count)
    ).astype(jnp.bfloat16)
    tall_block = lax.all_gather(merged, "orb", axis=1, tiled=True)
    wide_block = lax.all_gather(merged, "ff", axis=2, tiled=True)
    half = jnp.einsum(
        "qrj,qji->qri", wide_block, bubble, preferred_element_type=jnp.float32
    ).astype(jnp.bfloat16)
    change = jnp.einsum("qri,qic->qrc", half, tall_block, preferred_element_type=jnp.float32)
    return (merged.astype(jnp.float32) + change).astype(jnp.bfloat16)


CHUNKS = 2
ENDS = 4


def body_line(vertex_own, vertex_cross, project_coeff, green_left, green_right, window, shifts):
    points, row_count, col_count = vertex_own.shape
    form_count = shifts.shape[0]
    pair_rows = row_count // form_count
    total_k = green_left.shape[1]
    place = lax.axis_index("mom")
    chunk_pairs = pair_rows // CHUNKS
    chunk_rows = chunk_pairs * form_count

    padded = jnp.pad(project_coeff, ((0, 0), (2 * points, 2 * points), (0, 0), (0, 0)))
    padded = padded.transpose(0, 2, 1, 3).reshape(points * form_count, -1)
    wide = points * form_count
    own_coeff = lax.dynamic_slice_in_dim(padded, place * wide, 5 * wide, 1)
    straight = padded[:, 2 * wide : 6 * wide]
    zero = jnp.zeros((wide, wide), straight.dtype)
    to_two = jnp.concatenate([straight[:, : 2 * wide], zero, zero, zero], axis=1)
    to_one = jnp.concatenate([zero, zero, zero, straight[:, 2 * wide :]], axis=1)
    end_coeff = lax.ppermute(jnp.where(place == 3, to_two, to_one), "mom", [(3, 2), (0, 1)])
    weights = jnp.concatenate([own_coeff, end_coeff], axis=0)
    weights = weights.reshape(2 * points, form_count, 5 * points, form_count)

    up = [(i, i + 1) for i in range(ENDS - 1)]
    down = [(i + 1, i) for i in range(ENDS - 1)]
    pieces = [
        vertex_cross[:, i * chunk_rows : (i + 1) * chunk_rows] for i in range(CHUNKS)
    ]
    below = [lax.ppermute(piece, "mom", up) for piece in pieces]
    above = [lax.ppermute(piece, "mom", down) for piece in pieces]
    far_below = [lax.ppermute(piece, "mom", [(1, 2)]) for piece in below]
    far_above = [lax.ppermute(piece, "mom", [(2, 1)]) for piece in above]

    my_window = lax.dynamic_slice_in_dim(window, place * points, points, 0)
    momenta = jnp.arange(total_k, dtype=jnp.int32)
    form_table = form_factors(shifts, momenta)
    half_pairs = green_left.shape[0] // 2
    first_left = jnp.where(
        lax.axis_index("ff") == 0, green_left, jnp.roll(green_left, half_pairs, axis=0)
    )
    first_right = jnp.where(
        lax.axis_index("orb") == 0, green_right, jnp.roll(green_right, half_pairs, axis=0)
    )
    left_loop = loop_left(first_left, form_table)
    right_loop = loop_right_all(first_right, form_table, momenta, my_window, total_k)
    bubble = jnp.einsum(
        "jk,qik->qji", left_loop, right_loop, preferred_element_type=jnp.float32
    ).astype(jnp.bfloat16)

    merged, halves, across = [], [], []
    swap = [(0, 1), (1, 0)]
    for i in range(CHUNKS):
        stack = jnp.concatenate([far_below[i], below[i], pieces[i], above[i], far_above[i]], axis=0)
        tiles = stack.reshape(5 * points, chunk_pairs, form_count, col_count)
        sums = jnp.einsum("qlpm,pamc->qalc", weights, tiles, preferred_element_type=jnp.float32)
        sums = sums.reshape(2 * points, chunk_rows, col_count)
        outer = lax.ppermute(sums[points:].astype(jnp.bfloat16), "mom", [(2, 3), (1, 0)])
        mine = vertex_own[:, i * chunk_rows : (i + 1) * chunk_rows].astype(jnp.float32)
        mine = (mine + sums[:points] + outer.astype(jnp.float32)).astype(jnp.bfloat16)
        merged.append(mine)
        across.append(lax.ppermute(mine, "orb", swap))
        beside = lax.ppermute(mine, "ff", swap)
        rows = jnp.concatenate([mine, beside], axis=2)
        halves.append(
            jnp.einsum(
                "qrj,qji->qri", rows, bubble, preferred_element_type=jnp.float32
            ).astype(jnp.bfloat16)
        )
    half = jnp.concatenate(halves, axis=1)
    tall = jnp.concatenate(merged + across, axis=1)
    change = jnp.einsum("qri,qic->qrc", half, tall, preferred_element_type=jnp.float32)
    total = jnp.concatenate(merged, axis=1).astype(jnp.float32) + change
    return total.astype(jnp.bfloat16)


def solution(mesh):
    sizes = dict(mesh.shape)
    in_line = sizes["mom"] == ENDS and sizes["orb"] == 2 and sizes["ff"] == 2
    return jax.shard_map(
        body_line if in_line else body_gathered,
        mesh=mesh,
        in_specs=(
            P(("grp", "mom"), "orb", "ff"),
            P(("grp", "mom"), "orb", "ff"),
            P("mom", None, None, None),
            P("grp", None),
            P("grp", None),
            P(),
            P(),
        ),
        out_specs=P(("grp", "mom"), "orb", "ff"),
        check_vma=False,
    )
```

```python
import math

import jax
import jax.numpy as jnp
from jax import lax
from jax.experimental import pallas as pl
from jax.experimental.pallas import tpu as pltpu
from jax.sharding import PartitionSpec as P

LX = 48


def form_factors(shifts, momenta):
    row_x = momenta // LX
    row_y = momenta % LX
    turn_count = (shifts[:, 0:1] * row_x[None, :] + shifts[:, 1:2] * row_y[None, :]) % LX
    phases = turn_count.astype(jnp.float32) * (2.0 * math.pi / LX)
    anchor = (shifts[:, 0] == 0) & (shifts[:, 1] == 0)
    weight = jnp.where(anchor, 1.0, math.sqrt(2.0)).astype(jnp.float32)
    return weight[:, None] * jnp.cos(phases)


def loop_left(green_part, form_table):
    loop_rows = green_part[:, None, :] * form_table[None, :, :]
    return loop_rows.reshape(-1, form_table.shape[1]).astype(jnp.bfloat16)


def shifted(doubled, momenta, qpoint, total_count):
    pairs = doubled.shape[0]
    step_y = qpoint % LX
    straight = lax.dynamic_slice(doubled, (0, qpoint), (pairs, total_count))
    back = (qpoint - LX + total_count) % total_count
    wrapped = lax.dynamic_slice(doubled, (0, back), (pairs, total_count))
    return jnp.where(momenta[None, :] % LX + step_y < LX, straight, wrapped)


def loop_right_all(green_right, form_table, momenta, qpoints, total_count):
    doubled = jnp.concatenate([green_right, green_right], axis=1)
    picked = jnp.stack(
        [shifted(doubled, momenta, qpoints[i], total_count) for i in range(qpoints.shape[0])]
    )
    loop_rows = picked[:, :, None, :] * form_table[None, None, :, :] * (1.0 / total_count)
    return loop_rows.reshape(qpoints.shape[0], -1, momenta.shape[0]).astype(jnp.bfloat16)


def body_gathered(vertex_own, vertex_cross, project_coeff, green_left, green_right, window, shifts):
    points, row_count, col_count = vertex_own.shape
    form_count = shifts.shape[0]
    pair_rows = row_count // form_count
    total_k = green_left.shape[1]
    my_start = lax.axis_index("mom") * points
    my_window = lax.dynamic_slice_in_dim(window, my_start, points, 0)
    arrived = lax.all_gather(vertex_cross, "mom", axis=0, tiled=True)
    momenta = jnp.arange(total_k, dtype=jnp.int32)
    form_table = form_factors(shifts, momenta)
    left_loop = loop_left(green_left, form_table)
    right_loop = loop_right_all(green_right, form_table, momenta, my_window, total_k)
    bubble = jnp.einsum(
        "jk,qik->qji", left_loop, right_loop, preferred_element_type=jnp.float32
    ).astype(jnp.bfloat16)
    count = arrived.shape[0]
    tiles = arrived.reshape(count, pair_rows, form_count, col_count)
    projected = jnp.einsum(
        "qplm,pamc->qalc", project_coeff, tiles, preferred_element_type=jnp.float32
    )
    merged = (
        vertex_own.astype(jnp.float32) + projected.reshape(points, row_count, col_count)
    ).astype(jnp.bfloat16)
    tall_block = lax.all_gather(merged, "orb", axis=1, tiled=True)
    wide_block = lax.all_gather(merged, "ff", axis=2, tiled=True)
    half = jnp.einsum(
        "qrj,qji->qri", wide_block, bubble, preferred_element_type=jnp.float32
    ).astype(jnp.bfloat16)
    change = jnp.einsum("qri,qic->qrc", half, tall_block, preferred_element_type=jnp.float32)
    return (merged.astype(jnp.float32) + change).astype(jnp.bfloat16)


def pick_kernel(window_ref, column_ref, green_ref, picked_ref):
    qpoint = window_ref[pl.program_id(0)]
    values = green_ref[...]
    total_count = values.shape[1]
    straight = pltpu.roll(values, lax.rem(total_count - qpoint, total_count), 1)
    wrapped = pltpu.roll(values, lax.rem(total_count - qpoint + LX, total_count), 1)
    stays = column_ref[...] + lax.rem(qpoint, LX) < LX
    picked_ref[0] = jnp.where(stays, straight, wrapped)


def pick_all(green, column, qpoints):
    pairs, total_k = green.shape
    points = qpoints.shape[0]
    return pl.pallas_call(
        pick_kernel,
        grid=(points,),
        out_shape=jax.ShapeDtypeStruct((points, pairs, total_k), jnp.float32),
        in_specs=[
            pl.BlockSpec(memory_space=pltpu.SMEM),
            pl.BlockSpec((1, total_k), lambda i: (0, 0)),
            pl.BlockSpec((pairs, total_k), lambda i: (0, 0)),
        ],
        out_specs=pl.BlockSpec((1, pairs, total_k), lambda i: (i, 0, 0)),
        compiler_params=pltpu.CompilerParams(vmem_limit_bytes=8 * 1024 * 1024),
        cost_estimate=pl.CostEstimate(
            flops=4 * points * pairs * total_k,
            bytes_accessed=8 * points * pairs * total_k,
            transcendentals=0,
        ),
    )(qpoints, column, green)


CHUNKS = 2
ENDS = 4


def body_line(vertex_own, vertex_cross, project_coeff, green_left, green_right, window, shifts):
    points, row_count, col_count = vertex_own.shape
    form_count = shifts.shape[0]
    pair_rows = row_count // form_count
    total_k = green_left.shape[1]
    place = lax.axis_index("mom")
    chunk_pairs = pair_rows // CHUNKS
    chunk_rows = chunk_pairs * form_count

    padded = jnp.pad(project_coeff, ((0, 0), (2 * points, 2 * points), (0, 0), (0, 0)))
    padded = padded.transpose(0, 2, 1, 3).reshape(points * form_count, -1)
    wide = points * form_count
    own_coeff = lax.dynamic_slice_in_dim(padded, place * wide, 5 * wide, 1)
    straight = padded[:, 2 * wide : 6 * wide]
    zero = jnp.zeros((wide, wide), straight.dtype)
    to_two = jnp.concatenate([straight[:, : 2 * wide], zero, zero, zero], axis=1)
    to_one = jnp.concatenate([zero, zero, zero, straight[:, 2 * wide :]], axis=1)
    end_coeff = lax.ppermute(jnp.where(place == 3, to_two, to_one), "mom", [(3, 2), (0, 1)])
    weights = jnp.concatenate([own_coeff, end_coeff], axis=0)
    weights = weights.reshape(2 * points, form_count, 5 * points, form_count)

    up = [(i, i + 1) for i in range(ENDS - 1)]
    down = [(i + 1, i) for i in range(ENDS - 1)]
    pieces = [
        vertex_cross[:, i * chunk_rows : (i + 1) * chunk_rows] for i in range(CHUNKS)
    ]
    below = [lax.ppermute(piece, "mom", up) for piece in pieces]
    above = [lax.ppermute(piece, "mom", down) for piece in pieces]
    my_window = lax.dynamic_slice_in_dim(window, place * points, points, 0)
    momenta = jnp.arange(total_k, dtype=jnp.int32)
    form_table = form_factors(shifts, momenta)
    half_pairs = green_left.shape[0] // 2
    first_left = jnp.where(
        lax.axis_index("ff") == 0, green_left, jnp.roll(green_left, half_pairs, axis=0)
    )
    first_right = jnp.where(
        lax.axis_index("orb") == 0, green_right, jnp.roll(green_right, half_pairs, axis=0)
    )
    left_loop = loop_left(first_left, form_table)
    picked = pick_all(first_right, (momenta % LX)[None, :], my_window)
    picked, below[0], above[0] = lax.optimization_barrier((picked, below[0], above[0]))
    far_below = [lax.ppermute(below[0], "mom", [(1, 2)])]
    far_above = [lax.ppermute(above[0], "mom", [(2, 1)])]
    right_loop = picked[:, :, None, :] * form_table[None, None, :, :] * (1.0 / total_k)
    right_loop = right_loop.reshape(points, -1, total_k).astype(jnp.bfloat16)
    right_loop, *rest = lax.optimization_barrier((right_loop, *below[1:], *above[1:]))
    below[1:], above[1:] = rest[: CHUNKS - 1], rest[CHUNKS - 1 :]
    far_below += [lax.ppermute(piece, "mom", [(1, 2)]) for piece in below[1:]]
    far_above += [lax.ppermute(piece, "mom", [(2, 1)]) for piece in above[1:]]
    bubble = jnp.einsum(
        "jk,qik->qji", left_loop, right_loop, preferred_element_type=jnp.float32
    ).astype(jnp.bfloat16)
    bubble, far_below[0], far_above[0] = lax.optimization_barrier(
        (bubble, far_below[0], far_above[0])
    )

    merged, halves, across = [], [], []
    swap = [(0, 1), (1, 0)]
    for i in range(CHUNKS):
        stack = jnp.concatenate([far_below[i], below[i], pieces[i], above[i], far_above[i]], axis=0)
        tiles = stack.reshape(5 * points, chunk_pairs, form_count, col_count)
        sums = jnp.einsum("qlpm,pamc->qalc", weights, tiles, preferred_element_type=jnp.float32)
        sums = sums.reshape(2 * points, chunk_rows, col_count)
        outer = lax.ppermute(sums[points:].astype(jnp.bfloat16), "mom", [(2, 3), (1, 0)])
        mine = vertex_own[:, i * chunk_rows : (i + 1) * chunk_rows].astype(jnp.float32)
        mine = (mine + sums[:points] + outer.astype(jnp.float32)).astype(jnp.bfloat16)
        merged.append(mine)
        across.append(lax.ppermute(mine, "orb", swap))
        beside = lax.ppermute(mine, "ff", swap)
        rows = jnp.concatenate([mine, beside], axis=2)
        halves.append(
            jnp.einsum(
                "qrj,qji->qri", rows, bubble, preferred_element_type=jnp.float32
            ).astype(jnp.bfloat16)
        )
    half = jnp.concatenate(halves, axis=1)
    tall = jnp.concatenate(merged + across, axis=1)
    change = jnp.einsum("qri,qic->qrc", half, tall, preferred_element_type=jnp.float32)
    total = jnp.concatenate(merged, axis=1).astype(jnp.float32) + change
    return total.astype(jnp.bfloat16)


def solution(mesh):
    sizes = dict(mesh.shape)
    in_line = sizes["mom"] == ENDS and sizes["orb"] == 2 and sizes["ff"] == 2
    return jax.shard_map(
        body_line if in_line else body_gathered,
        mesh=mesh,
        in_specs=(
            P(("grp", "mom"), "orb", "ff"),
            P(("grp", "mom"), "orb", "ff"),
            P("mom", None, None, None),
            P("grp", None),
            P("grp", None),
            P(),
            P(),
        ),
        out_specs=P(("grp", "mom"), "orb", "ff"),
        check_vma=False,
    )
```

```python
import math

import jax
import jax.numpy as jnp
from jax import lax
from jax.experimental import pallas as pl
from jax.experimental.pallas import tpu as pltpu
from jax.sharding import PartitionSpec as P

LX = 48


def form_factors(shifts, momenta):
    row_x = momenta // LX
    row_y = momenta % LX
    turn_count = (shifts[:, 0:1] * row_x[None, :] + shifts[:, 1:2] * row_y[None, :]) % LX
    phases = turn_count.astype(jnp.float32) * (2.0 * math.pi / LX)
    anchor = (shifts[:, 0] == 0) & (shifts[:, 1] == 0)
    weight = jnp.where(anchor, 1.0, math.sqrt(2.0)).astype(jnp.float32)
    return weight[:, None] * jnp.cos(phases)


def loop_left(green_part, form_table):
    loop_rows = green_part[:, None, :] * form_table[None, :, :]
    return loop_rows.reshape(-1, form_table.shape[1]).astype(jnp.bfloat16)


def shifted(doubled, momenta, qpoint, total_count):
    pairs = doubled.shape[0]
    step_y = qpoint % LX
    straight = lax.dynamic_slice(doubled, (0, qpoint), (pairs, total_count))
    back = (qpoint - LX + total_count) % total_count
    wrapped = lax.dynamic_slice(doubled, (0, back), (pairs, total_count))
    return jnp.where(momenta[None, :] % LX + step_y < LX, straight, wrapped)


def loop_right_all(green_right, form_table, momenta, qpoints, total_count):
    doubled = jnp.concatenate([green_right, green_right], axis=1)
    picked = jnp.stack(
        [shifted(doubled, momenta, qpoints[i], total_count) for i in range(qpoints.shape[0])]
    )
    loop_rows = picked[:, :, None, :] * form_table[None, None, :, :] * (1.0 / total_count)
    return loop_rows.reshape(qpoints.shape[0], -1, momenta.shape[0]).astype(jnp.bfloat16)


def body_gathered(vertex_own, vertex_cross, project_coeff, green_left, green_right, window, shifts):
    points, row_count, col_count = vertex_own.shape
    form_count = shifts.shape[0]
    pair_rows = row_count // form_count
    total_k = green_left.shape[1]
    my_start = lax.axis_index("mom") * points
    my_window = lax.dynamic_slice_in_dim(window, my_start, points, 0)
    arrived = lax.all_gather(vertex_cross, "mom", axis=0, tiled=True)
    momenta = jnp.arange(total_k, dtype=jnp.int32)
    form_table = form_factors(shifts, momenta)
    left_loop = loop_left(green_left, form_table)
    right_loop = loop_right_all(green_right, form_table, momenta, my_window, total_k)
    bubble = jnp.einsum(
        "jk,qik->qji", left_loop, right_loop, preferred_element_type=jnp.float32
    ).astype(jnp.bfloat16)
    count = arrived.shape[0]
    tiles = arrived.reshape(count, pair_rows, form_count, col_count)
    projected = jnp.einsum(
        "qplm,pamc->qalc", project_coeff, tiles, preferred_element_type=jnp.float32
    )
    merged = (
        vertex_own.astype(jnp.float32) + projected.reshape(points, row_count, col_count)
    ).astype(jnp.bfloat16)
    tall_block = lax.all_gather(merged, "orb", axis=1, tiled=True)
    wide_block = lax.all_gather(merged, "ff", axis=2, tiled=True)
    half = jnp.einsum(
        "qrj,qji->qri", wide_block, bubble, preferred_element_type=jnp.float32
    ).astype(jnp.bfloat16)
    change = jnp.einsum("qri,qic->qrc", half, tall_block, preferred_element_type=jnp.float32)
    return (merged.astype(jnp.float32) + change).astype(jnp.bfloat16)


def three_parts(values):
    high = values.astype(jnp.bfloat16).astype(jnp.float32)
    rest = values - high
    middle = rest.astype(jnp.bfloat16).astype(jnp.float32)
    return jnp.concatenate([high, middle, rest - middle], axis=0).astype(jnp.bfloat16)


def spread(one_hot, values):
    return jnp.dot(one_hot, three_parts(values), preferred_element_type=jnp.float32)


def loop_kernel(
    window_ref, column_ref, left_ref, right_ref, form_ref, rows_l, rows_r, rows_f, out_ref,
    loop_l, form_all,
):
    @pl.when(pl.program_id(0) == 0)
    def _():
        form_all[...] = spread(rows_f[...], form_ref[...])
        loop_l[...] = (spread(rows_l[...], left_ref[...]) * form_all[...]).astype(jnp.bfloat16)

    qpoint = window_ref[pl.program_id(0)]
    values = right_ref[...]
    total_k = values.shape[1]
    straight = pltpu.roll(values, lax.rem(total_k - qpoint, total_k), 1)
    wrapped = pltpu.roll(values, lax.rem(total_k - qpoint + LX, total_k), 1)
    stays = column_ref[...] + lax.rem(qpoint, LX) < LX
    picked = spread(rows_r[...], jnp.where(stays, straight, wrapped))
    loop_r = (picked * form_all[...] * (1.0 / total_k)).astype(jnp.bfloat16)
    product = lax.dot_general(
        loop_l[...], loop_r, (((1,), (1,)), ((), ())), preferred_element_type=jnp.float32
    )
    out_ref[0] = product.astype(jnp.bfloat16)


def padded_rows(values, step):
    return jnp.pad(values, ((0, -values.shape[0] % step), (0, 0)))


def one_hot_rows(index, height):
    places = jnp.arange(3 * height, dtype=jnp.int32) % height
    return (index[:, None] == places[None, :]).astype(jnp.bfloat16)


def loop_matrices(qpoints, column, left, right, form, rows_l, rows_r, rows_f):
    points = qpoints.shape[0]
    order = rows_l.shape[0]
    total_k = left.shape[1]
    whole = [column, left, right, form, rows_l, rows_r, rows_f]
    return pl.pallas_call(
        loop_kernel,
        grid=(points,),
        out_shape=jax.ShapeDtypeStruct((points, order, order), jnp.bfloat16),
        in_specs=[pl.BlockSpec(memory_space=pltpu.SMEM)]
        + [pl.BlockSpec(each.shape, lambda i: (0, 0)) for each in whole],
        out_specs=pl.BlockSpec((1, order, order), lambda i: (i, 0, 0)),
        scratch_shapes=[
            pltpu.VMEM((order, total_k), jnp.bfloat16),
            pltpu.VMEM((order, total_k), jnp.float32),
        ],
        compiler_params=pltpu.CompilerParams(vmem_limit_bytes=36 * 1024 * 1024),
        cost_estimate=pl.CostEstimate(flops=1000, bytes_accessed=1000, transcendentals=0),
    )(qpoints, *whole)


CHUNKS = 2
ENDS = 4


def body_line(vertex_own, vertex_cross, project_coeff, green_left, green_right, window, shifts):
    points, row_count, col_count = vertex_own.shape
    form_count = shifts.shape[0]
    pair_rows = row_count // form_count
    total_k = green_left.shape[1]
    place = lax.axis_index("mom")
    chunk_pairs = pair_rows // CHUNKS
    chunk_rows = chunk_pairs * form_count

    padded = jnp.pad(project_coeff, ((0, 0), (2 * points, 2 * points), (0, 0), (0, 0)))
    padded = padded.transpose(0, 2, 1, 3).reshape(points * form_count, -1)
    wide = points * form_count
    own_coeff = lax.dynamic_slice_in_dim(padded, place * wide, 5 * wide, 1)
    straight = padded[:, 2 * wide : 6 * wide]
    zero = jnp.zeros((wide, wide), straight.dtype)
    to_two = jnp.concatenate([straight[:, : 2 * wide], zero, zero, zero], axis=1)
    to_one = jnp.concatenate([zero, zero, zero, straight[:, 2 * wide :]], axis=1)
    end_coeff = lax.ppermute(jnp.where(place == 3, to_two, to_one), "mom", [(3, 2), (0, 1)])
    weights = jnp.concatenate([own_coeff, end_coeff], axis=0)
    weights = weights.reshape(2 * points, form_count, 5 * points, form_count)

    up = [(i, i + 1) for i in range(ENDS - 1)]
    down = [(i + 1, i) for i in range(ENDS - 1)]
    pieces = [
        vertex_cross[:, i * chunk_rows : (i + 1) * chunk_rows] for i in range(CHUNKS)
    ]
    below = [lax.ppermute(piece, "mom", up) for piece in pieces]
    above = [lax.ppermute(piece, "mom", down) for piece in pieces]
    my_window = lax.dynamic_slice_in_dim(window, place * points, points, 0)
    momenta = jnp.arange(total_k, dtype=jnp.int32)
    form_table = form_factors(shifts, momenta)
    all_pairs = green_left.shape[0]
    left = padded_rows(green_left, 8)
    right = padded_rows(green_right, 8)
    form = padded_rows(form_table, 8)
    order = jnp.arange(all_pairs * form_count, dtype=jnp.int32)
    my_col = lax.axis_index("ff") * (all_pairs // 2)
    my_row = lax.axis_index("orb") * (all_pairs // 2)
    rows_l = one_hot_rows((order // form_count + my_col) % all_pairs, left.shape[0])
    rows_r = one_hot_rows((order // form_count + my_row) % all_pairs, right.shape[0])
    rows_f = one_hot_rows(order % form_count, form.shape[0])
    column = (momenta % LX)[None, :]
    cut = points // 2
    tables = (left, right, form, rows_l, rows_r, rows_f)
    right, below[0], above[0] = lax.optimization_barrier((right, below[0], above[0]))
    far_below = [lax.ppermute(below[0], "mom", [(1, 2)])]
    far_above = [lax.ppermute(above[0], "mom", [(2, 1)])]
    first = loop_matrices(my_window[:cut], column, left, right, *tables[2:])
    first, right, *rest = lax.optimization_barrier((first, right, *below[1:], *above[1:]))
    below[1:], above[1:] = rest[: CHUNKS - 1], rest[CHUNKS - 1 :]
    far_below += [lax.ppermute(piece, "mom", [(1, 2)]) for piece in below[1:]]
    far_above += [lax.ppermute(piece, "mom", [(2, 1)]) for piece in above[1:]]
    second = loop_matrices(my_window[cut:], column, left, right, *tables[2:])
    first, second, far_below[0], far_above[0] = lax.optimization_barrier(
        (first, second, far_below[0], far_above[0])
    )
    bubble = (first, second)

    merged, halves, across = [], [], []
    swap = [(0, 1), (1, 0)]
    for i in range(CHUNKS):
        stack = jnp.concatenate([far_below[i], below[i], pieces[i], above[i], far_above[i]], axis=0)
        tiles = stack.reshape(5 * points, chunk_pairs, form_count, col_count)
        sums = jnp.einsum("qlpm,pamc->qalc", weights, tiles, preferred_element_type=jnp.float32)
        sums = sums.reshape(2 * points, chunk_rows, col_count)
        outer = lax.ppermute(sums[points:].astype(jnp.bfloat16), "mom", [(2, 3), (1, 0)])
        mine = vertex_own[:, i * chunk_rows : (i + 1) * chunk_rows].astype(jnp.float32)
        mine = (mine + sums[:points] + outer.astype(jnp.float32)).astype(jnp.bfloat16)
        merged.append(mine)
        across.append(lax.ppermute(mine, "orb", swap))
        beside = lax.ppermute(mine, "ff", swap)
        rows = jnp.concatenate([mine, beside], axis=2)
        parts = [
            jnp.einsum("qrj,qji->qri", part, loops, preferred_element_type=jnp.float32)
            for part, loops in zip((rows[:cut], rows[cut:]), bubble)
        ]
        halves.append(jnp.concatenate(parts, axis=0).astype(jnp.bfloat16))
    half = jnp.concatenate(halves, axis=1)
    tall = jnp.concatenate(merged + across, axis=1)
    change = jnp.einsum("qri,qic->qrc", half, tall, preferred_element_type=jnp.float32)
    total = jnp.concatenate(merged, axis=1).astype(jnp.float32) + change
    return total.astype(jnp.bfloat16)


def solution(mesh):
    sizes = dict(mesh.shape)
    in_line = sizes["mom"] == ENDS and sizes["orb"] == 2 and sizes["ff"] == 2
    return jax.shard_map(
        body_line if in_line else body_gathered,
        mesh=mesh,
        in_specs=(
            P(("grp", "mom"), "orb", "ff"),
            P(("grp", "mom"), "orb", "ff"),
            P("mom", None, None, None),
            P("grp", None),
            P("grp", None),
            P(),
            P(),
        ),
        out_specs=P(("grp", "mom"), "orb", "ff"),
        check_vma=False,
    )
```

```python
import math

import jax
import jax.numpy as jnp
from jax import lax
from jax.experimental import pallas as pl
from jax.experimental.pallas import tpu as pltpu
from jax.sharding import PartitionSpec as P

LX = 48


def form_factors(shifts, momenta):
    row_x = momenta // LX
    row_y = momenta % LX
    turn_count = (shifts[:, 0:1] * row_x[None, :] + shifts[:, 1:2] * row_y[None, :]) % LX
    phases = turn_count.astype(jnp.float32) * (2.0 * math.pi / LX)
    anchor = (shifts[:, 0] == 0) & (shifts[:, 1] == 0)
    weight = jnp.where(anchor, 1.0, math.sqrt(2.0)).astype(jnp.float32)
    return weight[:, None] * jnp.cos(phases)


def loop_left(green_part, form_table):
    loop_rows = green_part[:, None, :] * form_table[None, :, :]
    return loop_rows.reshape(-1, form_table.shape[1]).astype(jnp.bfloat16)


def shifted(doubled, momenta, qpoint, total_count):
    pairs = doubled.shape[0]
    step_y = qpoint % LX
    straight = lax.dynamic_slice(doubled, (0, qpoint), (pairs, total_count))
    back = (qpoint - LX + total_count) % total_count
    wrapped = lax.dynamic_slice(doubled, (0, back), (pairs, total_count))
    return jnp.where(momenta[None, :] % LX + step_y < LX, straight, wrapped)


def loop_right_all(green_right, form_table, momenta, qpoints, total_count):
    doubled = jnp.concatenate([green_right, green_right], axis=1)
    picked = jnp.stack(
        [shifted(doubled, momenta, qpoints[i], total_count) for i in range(qpoints.shape[0])]
    )
    loop_rows = picked[:, :, None, :] * form_table[None, None, :, :] * (1.0 / total_count)
    return loop_rows.reshape(qpoints.shape[0], -1, momenta.shape[0]).astype(jnp.bfloat16)


def body_gathered(vertex_own, vertex_cross, project_coeff, green_left, green_right, window, shifts):
    points, row_count, col_count = vertex_own.shape
    form_count = shifts.shape[0]
    pair_rows = row_count // form_count
    total_k = green_left.shape[1]
    my_start = lax.axis_index("mom") * points
    my_window = lax.dynamic_slice_in_dim(window, my_start, points, 0)
    arrived = lax.all_gather(vertex_cross, "mom", axis=0, tiled=True)
    momenta = jnp.arange(total_k, dtype=jnp.int32)
    form_table = form_factors(shifts, momenta)
    left_loop = loop_left(green_left, form_table)
    right_loop = loop_right_all(green_right, form_table, momenta, my_window, total_k)
    bubble = jnp.einsum(
        "jk,qik->qji", left_loop, right_loop, preferred_element_type=jnp.float32
    ).astype(jnp.bfloat16)
    count = arrived.shape[0]
    tiles = arrived.reshape(count, pair_rows, form_count, col_count)
    projected = jnp.einsum(
        "qplm,pamc->qalc", project_coeff, tiles, preferred_element_type=jnp.float32
    )
    merged = (
        vertex_own.astype(jnp.float32) + projected.reshape(points, row_count, col_count)
    ).astype(jnp.bfloat16)
    tall_block = lax.all_gather(merged, "orb", axis=1, tiled=True)
    wide_block = lax.all_gather(merged, "ff", axis=2, tiled=True)
    half = jnp.einsum(
        "qrj,qji->qri", wide_block, bubble, preferred_element_type=jnp.float32
    ).astype(jnp.bfloat16)
    change = jnp.einsum("qri,qic->qrc", half, tall_block, preferred_element_type=jnp.float32)
    return (merged.astype(jnp.float32) + change).astype(jnp.bfloat16)


def three_parts(values):
    high = values.astype(jnp.bfloat16).astype(jnp.float32)
    rest = values - high
    middle = rest.astype(jnp.bfloat16).astype(jnp.float32)
    return jnp.concatenate([high, middle, rest - middle], axis=0).astype(jnp.bfloat16)


def spread(one_hot, values):
    return jnp.dot(one_hot, three_parts(values), preferred_element_type=jnp.float32)


def loop_kernel(
    window_ref, column_ref, left_ref, right_ref, form_ref, rows_l, rows_r, rows_f, out_ref,
    loop_l, form_all,
):
    @pl.when(pl.program_id(0) == 0)
    def _():
        form_all[...] = spread(rows_f[...], form_ref[...])
        loop_l[...] = (spread(rows_l[...], left_ref[...]) * form_all[...]).astype(jnp.bfloat16)

    qpoint = window_ref[pl.program_id(0)]
    values = right_ref[...]
    total_k = values.shape[1]
    straight = pltpu.roll(values, lax.rem(total_k - qpoint, total_k), 1)
    wrapped = pltpu.roll(values, lax.rem(total_k - qpoint + LX, total_k), 1)
    stays = column_ref[...] + lax.rem(qpoint, LX) < LX
    picked = spread(rows_r[...], jnp.where(stays, straight, wrapped))
    loop_r = (picked * form_all[...] * (1.0 / total_k)).astype(jnp.bfloat16)
    product = lax.dot_general(
        loop_l[...], loop_r, (((1,), (1,)), ((), ())), preferred_element_type=jnp.float32
    )
    out_ref[0] = product.astype(jnp.bfloat16)


def padded_rows(values, step):
    return jnp.pad(values, ((0, -values.shape[0] % step), (0, 0)))


def one_hot_rows(index, height):
    places = jnp.arange(3 * height, dtype=jnp.int32) % height
    return (index[:, None] == places[None, :]).astype(jnp.bfloat16)


def loop_matrices(qpoints, column, left, right, form, rows_l, rows_r, rows_f):
    points = qpoints.shape[0]
    order = rows_l.shape[0]
    total_k = left.shape[1]
    whole = [column, left, right, form, rows_l, rows_r, rows_f]
    return pl.pallas_call(
        loop_kernel,
        grid=(points,),
        out_shape=jax.ShapeDtypeStruct((points, order, order), jnp.bfloat16),
        in_specs=[pl.BlockSpec(memory_space=pltpu.SMEM)]
        + [pl.BlockSpec(each.shape, lambda i: (0, 0)) for each in whole],
        out_specs=pl.BlockSpec((1, order, order), lambda i: (i, 0, 0)),
        scratch_shapes=[
            pltpu.VMEM((order, total_k), jnp.bfloat16),
            pltpu.VMEM((order, total_k), jnp.float32),
        ],
        compiler_params=pltpu.CompilerParams(vmem_limit_bytes=36 * 1024 * 1024),
        cost_estimate=pl.CostEstimate(flops=1000, bytes_accessed=1000, transcendentals=0),
    )(qpoints, *whole)


CHUNKS = 2
ENDS = 4


def body_line(vertex_own, vertex_cross, project_coeff, green_left, green_right, window, shifts):
    points, row_count, col_count = vertex_own.shape
    form_count = shifts.shape[0]
    pair_rows = row_count // form_count
    total_k = green_left.shape[1]
    place = lax.axis_index("mom")
    chunk_pairs = pair_rows // CHUNKS
    chunk_rows = chunk_pairs * form_count

    padded = jnp.pad(project_coeff, ((0, 0), (2 * points, 2 * points), (0, 0), (0, 0)))
    own_coeff = lax.dynamic_slice_in_dim(padded, place * points, 5 * points, 1)
    near = 2 * points
    to_two = jnp.pad(project_coeff[:, :near], ((0, 0), (0, 3 * points), (0, 0), (0, 0)))
    to_one = jnp.pad(project_coeff[:, near:], ((0, 0), (3 * points, 0), (0, 0), (0, 0)))
    end_coeff = lax.ppermute(jnp.where(place == 3, to_two, to_one), "mom", [(3, 2), (0, 1)])
    weights = jnp.concatenate([own_coeff, end_coeff], axis=0)

    up = [(i, i + 1) for i in range(ENDS - 1)]
    down = [(i + 1, i) for i in range(ENDS - 1)]
    pieces = [
        vertex_cross[:, i * chunk_rows : (i + 1) * chunk_rows] for i in range(CHUNKS)
    ]
    below = [lax.ppermute(piece, "mom", up) for piece in pieces]
    above = [lax.ppermute(piece, "mom", down) for piece in pieces]
    my_window = lax.dynamic_slice_in_dim(window, place * points, points, 0)
    momenta = jnp.arange(total_k, dtype=jnp.int32)
    form_table = form_factors(shifts, momenta)
    all_pairs = green_left.shape[0]
    left = padded_rows(green_left, 8)
    right = padded_rows(green_right, 8)
    form = padded_rows(form_table, 8)
    order = jnp.arange(all_pairs * form_count, dtype=jnp.int32)
    my_col = lax.axis_index("ff") * (all_pairs // 2)
    my_row = lax.axis_index("orb") * (all_pairs // 2)
    rows_l = one_hot_rows((order // form_count + my_col) % all_pairs, left.shape[0])
    rows_r = one_hot_rows((order // form_count + my_row) % all_pairs, right.shape[0])
    rows_f = one_hot_rows(order % form_count, form.shape[0])
    column = (momenta % LX)[None, :]
    tables = (form, rows_l, rows_r, rows_f)
    bounds = [0, points // 2, points * 3 // 4, points]
    spans = list(zip(bounds[:-1], bounds[1:]))
    parts = [my_window[lo:hi] for lo, hi in spans]
    right, below, above = lax.optimization_barrier((right, below, above))
    far_below = [lax.ppermute(piece, "mom", [(1, 2)]) for piece in below]
    far_above = [lax.ppermute(piece, "mom", [(2, 1)]) for piece in above]
    loops = [loop_matrices(parts[0], column, left, right, *tables)]
    weights, loops[0] = lax.optimization_barrier((weights, loops[0]))

    sums, sent = [], []
    for i in range(CHUNKS):
        stack = jnp.concatenate([far_below[i], below[i], pieces[i], above[i], far_above[i]], axis=0)
        tiles = stack.reshape(5 * points, chunk_pairs, form_count, col_count)
        both = jnp.einsum("qplm,pamc->qalc", weights, tiles, preferred_element_type=jnp.float32)
        both = both.reshape(2 * points, chunk_rows, col_count)
        sums.append(both[:points])
        sent.append(both[points:].astype(jnp.bfloat16))
        if i + 1 < CHUNKS:
            sent[i], far_below[i + 1], far_above[i + 1] = lax.optimization_barrier(
                (sent[i], far_below[i + 1], far_above[i + 1])
            )
    sent[-1], right = lax.optimization_barrier((sent[-1], right))
    outer = [lax.ppermute(each, "mom", [(2, 3), (1, 0)]) for each in sent]
    loops.append(loop_matrices(parts[1], column, left, right, *tables))

    merged, halves, across, beside = [], [], [], []
    swap = [(0, 1), (1, 0)]
    for i in range(CHUNKS):
        mine = vertex_own[:, i * chunk_rows : (i + 1) * chunk_rows].astype(jnp.float32)
        if i == 0:
            outer[0], loops[1] = lax.optimization_barrier((outer[0], loops[1]))
        mine = (mine + sums[i] + outer[i].astype(jnp.float32)).astype(jnp.bfloat16)
        if i == 0:
            mine, right = lax.optimization_barrier((mine, right))
            loops.append(loop_matrices(parts[2], column, left, right, *tables))
        merged.append(mine)
        across.append(lax.ppermute(mine, "orb", swap))
        beside.append(lax.ppermute(mine, "ff", swap))
    for i in range(CHUNKS):
        rows = jnp.concatenate([merged[i], beside[i]], axis=2)
        terms = [
            jnp.einsum("qrj,qji->qri", rows[lo:hi], loop, preferred_element_type=jnp.float32)
            for (lo, hi), loop in zip(spans, loops)
        ]
        halves.append(jnp.concatenate(terms, axis=0).astype(jnp.bfloat16))
    half = jnp.concatenate(halves, axis=1)
    tall = jnp.concatenate(merged + across, axis=1)
    change = jnp.einsum("qri,qic->qrc", half, tall, preferred_element_type=jnp.float32)
    total = jnp.concatenate(merged, axis=1).astype(jnp.float32) + change
    return total.astype(jnp.bfloat16)


def solution(mesh):
    sizes = dict(mesh.shape)
    in_line = sizes["mom"] == ENDS and sizes["orb"] == 2 and sizes["ff"] == 2
    return jax.shard_map(
        body_line if in_line else body_gathered,
        mesh=mesh,
        in_specs=(
            P(("grp", "mom"), "orb", "ff"),
            P(("grp", "mom"), "orb", "ff"),
            P("mom", None, None, None),
            P("grp", None),
            P("grp", None),
            P(),
            P(),
        ),
        out_specs=P(("grp", "mom"), "orb", "ff"),
        check_vma=False,
    )
```

```python
import math

import jax
import jax.numpy as jnp
from jax import lax
from jax.experimental import pallas as pl
from jax.experimental.pallas import tpu as pltpu
from jax.sharding import PartitionSpec as P

LX = 48


def form_factors(shifts, momenta):
    row_x = momenta // LX
    row_y = momenta % LX
    turn_count = (shifts[:, 0:1] * row_x[None, :] + shifts[:, 1:2] * row_y[None, :]) % LX
    phases = turn_count.astype(jnp.float32) * (2.0 * math.pi / LX)
    anchor = (shifts[:, 0] == 0) & (shifts[:, 1] == 0)
    weight = jnp.where(anchor, 1.0, math.sqrt(2.0)).astype(jnp.float32)
    return weight[:, None] * jnp.cos(phases)


def loop_left(green_part, form_table):
    loop_rows = green_part[:, None, :] * form_table[None, :, :]
    return loop_rows.reshape(-1, form_table.shape[1]).astype(jnp.bfloat16)


def shifted(doubled, momenta, qpoint, total_count):
    pairs = doubled.shape[0]
    step_y = qpoint % LX
    straight = lax.dynamic_slice(doubled, (0, qpoint), (pairs, total_count))
    back = (qpoint - LX + total_count) % total_count
    wrapped = lax.dynamic_slice(doubled, (0, back), (pairs, total_count))
    return jnp.where(momenta[None, :] % LX + step_y < LX, straight, wrapped)


def loop_right_all(green_right, form_table, momenta, qpoints, total_count):
    doubled = jnp.concatenate([green_right, green_right], axis=1)
    picked = jnp.stack(
        [shifted(doubled, momenta, qpoints[i], total_count) for i in range(qpoints.shape[0])]
    )
    loop_rows = picked[:, :, None, :] * form_table[None, None, :, :] * (1.0 / total_count)
    return loop_rows.reshape(qpoints.shape[0], -1, momenta.shape[0]).astype(jnp.bfloat16)


def body_gathered(vertex_own, vertex_cross, project_coeff, green_left, green_right, window, shifts):
    points, row_count, col_count = vertex_own.shape
    form_count = shifts.shape[0]
    pair_rows = row_count // form_count
    total_k = green_left.shape[1]
    my_start = lax.axis_index("mom") * points
    my_window = lax.dynamic_slice_in_dim(window, my_start, points, 0)
    arrived = lax.all_gather(vertex_cross, "mom", axis=0, tiled=True)
    momenta = jnp.arange(total_k, dtype=jnp.int32)
    form_table = form_factors(shifts, momenta)
    left_loop = loop_left(green_left, form_table)
    right_loop = loop_right_all(green_right, form_table, momenta, my_window, total_k)
    bubble = jnp.einsum(
        "jk,qik->qji", left_loop, right_loop, preferred_element_type=jnp.float32
    ).astype(jnp.bfloat16)
    count = arrived.shape[0]
    tiles = arrived.reshape(count, pair_rows, form_count, col_count)
    projected = jnp.einsum(
        "qplm,pamc->qalc", project_coeff, tiles, preferred_element_type=jnp.float32
    )
    merged = (
        vertex_own.astype(jnp.float32) + projected.reshape(points, row_count, col_count)
    ).astype(jnp.bfloat16)
    tall_block = lax.all_gather(merged, "orb", axis=1, tiled=True)
    wide_block = lax.all_gather(merged, "ff", axis=2, tiled=True)
    half = jnp.einsum(
        "qrj,qji->qri", wide_block, bubble, preferred_element_type=jnp.float32
    ).astype(jnp.bfloat16)
    change = jnp.einsum("qri,qic->qrc", half, tall_block, preferred_element_type=jnp.float32)
    return (merged.astype(jnp.float32) + change).astype(jnp.bfloat16)


def three_parts(values):
    high = values.astype(jnp.bfloat16).astype(jnp.float32)
    rest = values - high
    middle = rest.astype(jnp.bfloat16).astype(jnp.float32)
    return jnp.concatenate([high, middle, rest - middle], axis=0).astype(jnp.bfloat16)


def spread(one_hot, values):
    return jnp.dot(one_hot, three_parts(values), preferred_element_type=jnp.float32)


def loop_kernel(
    window_ref, column_ref, left_ref, right_ref, form_ref, rows_l, rows_r, rows_f, out_ref,
    loop_l, form_all,
):
    @pl.when(pl.program_id(0) == 0)
    def _():
        form_all[...] = spread(rows_f[...], form_ref[...])
        loop_l[...] = (spread(rows_l[...], left_ref[...]) * form_all[...]).astype(jnp.bfloat16)

    qpoint = window_ref[pl.program_id(0)]
    values = right_ref[...]
    total_k = values.shape[1]
    straight = pltpu.roll(values, lax.rem(total_k - qpoint, total_k), 1)
    wrapped = pltpu.roll(values, lax.rem(total_k - qpoint + LX, total_k), 1)
    stays = column_ref[...] + lax.rem(qpoint, LX) < LX
    picked = spread(rows_r[...], jnp.where(stays, straight, wrapped))
    loop_r = (picked * form_all[...] * (1.0 / total_k)).astype(jnp.bfloat16)
    product = lax.dot_general(
        loop_l[...], loop_r, (((1,), (1,)), ((), ())), preferred_element_type=jnp.float32
    )
    out_ref[0] = product.astype(jnp.bfloat16)


def padded_rows(values, step):
    return jnp.pad(values, ((0, -values.shape[0] % step), (0, 0)))


def one_hot_rows(index, height):
    places = jnp.arange(3 * height, dtype=jnp.int32) % height
    return (index[:, None] == places[None, :]).astype(jnp.bfloat16)


def loop_matrices(qpoints, column, left, right, form, rows_l, rows_r, rows_f):
    points = qpoints.shape[0]
    order = rows_l.shape[0]
    total_k = left.shape[1]
    whole = [column, left, right, form, rows_l, rows_r, rows_f]
    return pl.pallas_call(
        loop_kernel,
        grid=(points,),
        out_shape=jax.ShapeDtypeStruct((points, order, order), jnp.bfloat16),
        in_specs=[pl.BlockSpec(memory_space=pltpu.SMEM)]
        + [pl.BlockSpec(each.shape, lambda i: (0, 0)) for each in whole],
        out_specs=pl.BlockSpec((1, order, order), lambda i: (i, 0, 0)),
        scratch_shapes=[
            pltpu.VMEM((order, total_k), jnp.bfloat16),
            pltpu.VMEM((order, total_k), jnp.float32),
        ],
        compiler_params=pltpu.CompilerParams(vmem_limit_bytes=36 * 1024 * 1024),
        cost_estimate=pl.CostEstimate(flops=1000, bytes_accessed=1000, transcendentals=0),
    )(qpoints, *whole)


CHUNKS = 2
ENDS = 4


def body_line(vertex_own, vertex_cross, project_coeff, green_left, green_right, window, shifts):
    points, row_count, col_count = vertex_own.shape
    form_count = shifts.shape[0]
    pair_rows = row_count // form_count
    total_k = green_left.shape[1]
    place = lax.axis_index("mom")
    chunk_pairs = pair_rows // CHUNKS
    chunk_rows = chunk_pairs * form_count

    padded = jnp.pad(project_coeff, ((0, 0), (2 * points, 2 * points), (0, 0), (0, 0)))
    own_coeff = lax.dynamic_slice_in_dim(padded, place * points, 5 * points, 1)
    near = 2 * points
    to_two = jnp.pad(project_coeff[:, :near], ((0, 0), (0, 3 * points), (0, 0), (0, 0)))
    to_one = jnp.pad(project_coeff[:, near:], ((0, 0), (3 * points, 0), (0, 0), (0, 0)))
    end_coeff = lax.ppermute(jnp.where(place == 3, to_two, to_one), "mom", [(3, 2), (0, 1)])
    weights = jnp.concatenate([own_coeff, end_coeff], axis=0)

    up = [(i, i + 1) for i in range(ENDS - 1)]
    down = [(i + 1, i) for i in range(ENDS - 1)]
    pieces = [
        vertex_cross[:, i * chunk_rows : (i + 1) * chunk_rows] for i in range(CHUNKS)
    ]
    below = [lax.ppermute(piece, "mom", up) for piece in pieces]
    above = [lax.ppermute(piece, "mom", down) for piece in pieces]
    my_window = lax.dynamic_slice_in_dim(window, place * points, points, 0)
    momenta = jnp.arange(total_k, dtype=jnp.int32)
    form_table = form_factors(shifts, momenta)
    all_pairs = green_left.shape[0]
    left = padded_rows(green_left, 8)
    right = padded_rows(green_right, 8)
    form = padded_rows(form_table, 8)
    order = jnp.arange(all_pairs * form_count, dtype=jnp.int32)
    my_col = lax.axis_index("ff") * (all_pairs // 2)
    my_row = lax.axis_index("orb") * (all_pairs // 2)
    rows_l = one_hot_rows((order // form_count + my_col) % all_pairs, left.shape[0])
    rows_r = one_hot_rows((order // form_count + my_row) % all_pairs, right.shape[0])
    rows_f = one_hot_rows(order % form_count, form.shape[0])
    column = (momenta % LX)[None, :]
    tables = (form, rows_l, rows_r, rows_f)
    bounds = [0, points // 2, points * 3 // 4, points]
    spans = list(zip(bounds[:-1], bounds[1:]))
    parts = [my_window[lo:hi] for lo, hi in spans]
    loops = [loop_matrices(parts[0], column, left, right, *tables)]
    loops, right, below, above = lax.optimization_barrier((loops, right, below, above))
    far_below = [lax.ppermute(piece, "mom", [(1, 2)]) for piece in below]
    far_above = [lax.ppermute(piece, "mom", [(2, 1)]) for piece in above]

    sums, sent = [], []
    for i in range(CHUNKS):
        stack = jnp.concatenate([far_below[i], below[i], pieces[i], above[i], far_above[i]], axis=0)
        tiles = stack.reshape(5 * points, chunk_pairs, form_count, col_count)
        both = jnp.einsum("qplm,pamc->qalc", weights, tiles, preferred_element_type=jnp.float32)
        both = both.reshape(2 * points, chunk_rows, col_count)
        sums.append(both[:points])
        sent.append(both[points:].astype(jnp.bfloat16))
    sent[-1], right = lax.optimization_barrier((sent[-1], right))
    outer = [lax.ppermute(each, "mom", [(2, 3), (1, 0)]) for each in sent]
    loops.append(loop_matrices(parts[1], column, left, right, *tables))

    merged, halves, across, beside = [], [], [], []
    swap = [(0, 1), (1, 0)]
    for i in range(CHUNKS):
        mine = vertex_own[:, i * chunk_rows : (i + 1) * chunk_rows].astype(jnp.float32)
        if i == 0:
            outer[0], loops[1] = lax.optimization_barrier((outer[0], loops[1]))
        mine = (mine + sums[i] + outer[i].astype(jnp.float32)).astype(jnp.bfloat16)
        if i == 0:
            mine, right = lax.optimization_barrier((mine, right))
            loops.append(loop_matrices(parts[2], column, left, right, *tables))
        merged.append(mine)
        across.append(lax.ppermute(mine, "orb", swap))
        beside.append(lax.ppermute(mine, "ff", swap))
    for i in range(CHUNKS):
        rows = jnp.concatenate([merged[i], beside[i]], axis=2)
        terms = [
            jnp.einsum("qrj,qji->qri", rows[lo:hi], loop, preferred_element_type=jnp.float32)
            for (lo, hi), loop in zip(spans, loops)
        ]
        halves.append(jnp.concatenate(terms, axis=0).astype(jnp.bfloat16))
    half = jnp.concatenate(halves, axis=1)
    tall = jnp.concatenate(merged + across, axis=1)
    change = jnp.einsum("qri,qic->qrc", half, tall, preferred_element_type=jnp.float32)
    total = jnp.concatenate(merged, axis=1).astype(jnp.float32) + change
    return total.astype(jnp.bfloat16)


def solution(mesh):
    sizes = dict(mesh.shape)
    in_line = sizes["mom"] == ENDS and sizes["orb"] == 2 and sizes["ff"] == 2
    return jax.shard_map(
        body_line if in_line else body_gathered,
        mesh=mesh,
        in_specs=(
            P(("grp", "mom"), "orb", "ff"),
            P(("grp", "mom"), "orb", "ff"),
            P("mom", None, None, None),
            P("grp", None),
            P("grp", None),
            P(),
            P(),
        ),
        out_specs=P(("grp", "mom"), "orb", "ff"),
        check_vma=False,
    )
```

```python
import math

import jax
import jax.numpy as jnp
from jax import lax
from jax.experimental import pallas as pl
from jax.experimental.pallas import tpu as pltpu
from jax.sharding import PartitionSpec as P

LX = 48


def form_factors(shifts, momenta):
    row_x = momenta // LX
    row_y = momenta % LX
    turn_count = (shifts[:, 0:1] * row_x[None, :] + shifts[:, 1:2] * row_y[None, :]) % LX
    phases = turn_count.astype(jnp.float32) * (2.0 * math.pi / LX)
    anchor = (shifts[:, 0] == 0) & (shifts[:, 1] == 0)
    weight = jnp.where(anchor, 1.0, math.sqrt(2.0)).astype(jnp.float32)
    return weight[:, None] * jnp.cos(phases)


def loop_left(green_part, form_table):
    loop_rows = green_part[:, None, :] * form_table[None, :, :]
    return loop_rows.reshape(-1, form_table.shape[1]).astype(jnp.bfloat16)


def shifted(doubled, momenta, qpoint, total_count):
    pairs = doubled.shape[0]
    step_y = qpoint % LX
    straight = lax.dynamic_slice(doubled, (0, qpoint), (pairs, total_count))
    back = (qpoint - LX + total_count) % total_count
    wrapped = lax.dynamic_slice(doubled, (0, back), (pairs, total_count))
    return jnp.where(momenta[None, :] % LX + step_y < LX, straight, wrapped)


def loop_right_all(green_right, form_table, momenta, qpoints, total_count):
    doubled = jnp.concatenate([green_right, green_right], axis=1)
    picked = jnp.stack(
        [shifted(doubled, momenta, qpoints[i], total_count) for i in range(qpoints.shape[0])]
    )
    loop_rows = picked[:, :, None, :] * form_table[None, None, :, :] * (1.0 / total_count)
    return loop_rows.reshape(qpoints.shape[0], -1, momenta.shape[0]).astype(jnp.bfloat16)


def body_gathered(vertex_own, vertex_cross, project_coeff, green_left, green_right, window, shifts):
    points, row_count, col_count = vertex_own.shape
    form_count = shifts.shape[0]
    pair_rows = row_count // form_count
    total_k = green_left.shape[1]
    my_start = lax.axis_index("mom") * points
    my_window = lax.dynamic_slice_in_dim(window, my_start, points, 0)
    arrived = lax.all_gather(vertex_cross, "mom", axis=0, tiled=True)
    momenta = jnp.arange(total_k, dtype=jnp.int32)
    form_table = form_factors(shifts, momenta)
    left_loop = loop_left(green_left, form_table)
    right_loop = loop_right_all(green_right, form_table, momenta, my_window, total_k)
    bubble = jnp.einsum(
        "jk,qik->qji", left_loop, right_loop, preferred_element_type=jnp.float32
    ).astype(jnp.bfloat16)
    count = arrived.shape[0]
    tiles = arrived.reshape(count, pair_rows, form_count, col_count)
    projected = jnp.einsum(
        "qplm,pamc->qalc", project_coeff, tiles, preferred_element_type=jnp.float32
    )
    merged = (
        vertex_own.astype(jnp.float32) + projected.reshape(points, row_count, col_count)
    ).astype(jnp.bfloat16)
    tall_block = lax.all_gather(merged, "orb", axis=1, tiled=True)
    wide_block = lax.all_gather(merged, "ff", axis=2, tiled=True)
    half = jnp.einsum(
        "qrj,qji->qri", wide_block, bubble, preferred_element_type=jnp.float32
    ).astype(jnp.bfloat16)
    change = jnp.einsum("qri,qic->qrc", half, tall_block, preferred_element_type=jnp.float32)
    return (merged.astype(jnp.float32) + change).astype(jnp.bfloat16)


def three_parts(values):
    high = values.astype(jnp.bfloat16).astype(jnp.float32)
    rest = values - high
    middle = rest.astype(jnp.bfloat16).astype(jnp.float32)
    return jnp.concatenate([high, middle, rest - middle], axis=0).astype(jnp.bfloat16)


def spread(one_hot, values):
    return jnp.dot(one_hot, three_parts(values), preferred_element_type=jnp.float32)


def loop_kernel(
    window_ref, column_ref, left_ref, right_ref, form_ref, rows_l, rows_r, rows_f, out_ref,
    loop_l, form_all,
):
    @pl.when(pl.program_id(0) == 0)
    def _():
        form_all[...] = spread(rows_f[...], form_ref[...])
        loop_l[...] = (spread(rows_l[...], left_ref[...]) * form_all[...]).astype(jnp.bfloat16)

    qpoint = window_ref[pl.program_id(0)]
    values = right_ref[...]
    total_k = values.shape[1]
    straight = pltpu.roll(values, lax.rem(total_k - qpoint, total_k), 1)
    wrapped = pltpu.roll(values, lax.rem(total_k - qpoint + LX, total_k), 1)
    stays = column_ref[...] + lax.rem(qpoint, LX) < LX
    picked = spread(rows_r[...], jnp.where(stays, straight, wrapped))
    loop_r = (picked * form_all[...] * (1.0 / total_k)).astype(jnp.bfloat16)
    product = lax.dot_general(
        loop_l[...], loop_r, (((1,), (1,)), ((), ())), preferred_element_type=jnp.float32
    )
    out_ref[0] = product.astype(jnp.bfloat16)


def padded_rows(values, step):
    return jnp.pad(values, ((0, -values.shape[0] % step), (0, 0)))


def one_hot_rows(index, height):
    places = jnp.arange(3 * height, dtype=jnp.int32) % height
    return (index[:, None] == places[None, :]).astype(jnp.bfloat16)


def loop_matrices(qpoints, column, left, right, form, rows_l, rows_r, rows_f):
    points = qpoints.shape[0]
    order = rows_l.shape[0]
    total_k = left.shape[1]
    whole = [column, left, right, form, rows_l, rows_r, rows_f]
    return pl.pallas_call(
        loop_kernel,
        grid=(points,),
        out_shape=jax.ShapeDtypeStruct((points, order, order), jnp.bfloat16),
        in_specs=[pl.BlockSpec(memory_space=pltpu.SMEM)]
        + [pl.BlockSpec(each.shape, lambda i: (0, 0)) for each in whole],
        out_specs=pl.BlockSpec((1, order, order), lambda i: (i, 0, 0)),
        scratch_shapes=[
            pltpu.VMEM((order, total_k), jnp.bfloat16),
            pltpu.VMEM((order, total_k), jnp.float32),
        ],
        compiler_params=pltpu.CompilerParams(vmem_limit_bytes=36 * 1024 * 1024),
        cost_estimate=pl.CostEstimate(flops=1000, bytes_accessed=1000, transcendentals=0),
    )(qpoints, *whole)


CHUNKS = 3
ENDS = 4


def body_line(vertex_own, vertex_cross, project_coeff, green_left, green_right, window, shifts):
    points, row_count, col_count = vertex_own.shape
    form_count = shifts.shape[0]
    pair_rows = row_count // form_count
    total_k = green_left.shape[1]
    place = lax.axis_index("mom")
    chunk_pairs = pair_rows // CHUNKS
    chunk_rows = chunk_pairs * form_count

    padded = jnp.pad(project_coeff, ((0, 0), (2 * points, 2 * points), (0, 0), (0, 0)))
    own_coeff = lax.dynamic_slice_in_dim(padded, place * points, 5 * points, 1)
    near = 2 * points
    to_two = jnp.pad(project_coeff[:, :near], ((0, 0), (0, 3 * points), (0, 0), (0, 0)))
    to_one = jnp.pad(project_coeff[:, near:], ((0, 0), (3 * points, 0), (0, 0), (0, 0)))
    end_coeff = lax.ppermute(jnp.where(place == 3, to_two, to_one), "mom", [(3, 2), (0, 1)])
    weights = jnp.concatenate([own_coeff, end_coeff], axis=0)

    up = [(i, i + 1) for i in range(ENDS - 1)]
    down = [(i + 1, i) for i in range(ENDS - 1)]
    pieces = [
        vertex_cross[:, i * chunk_rows : (i + 1) * chunk_rows] for i in range(CHUNKS)
    ]
    below = [lax.ppermute(piece, "mom", up) for piece in pieces]
    above = [lax.ppermute(piece, "mom", down) for piece in pieces]
    my_window = lax.dynamic_slice_in_dim(window, place * points, points, 0)
    momenta = jnp.arange(total_k, dtype=jnp.int32)
    form_table = form_factors(shifts, momenta)
    all_pairs = green_left.shape[0]
    left = padded_rows(green_left, 8)
    right = padded_rows(green_right, 8)
    form = padded_rows(form_table, 8)
    order = jnp.arange(all_pairs * form_count, dtype=jnp.int32)
    my_col = lax.axis_index("ff") * (all_pairs // 2)
    my_row = lax.axis_index("orb") * (all_pairs // 2)
    rows_l = one_hot_rows((order // form_count + my_col) % all_pairs, left.shape[0])
    rows_r = one_hot_rows((order // form_count + my_row) % all_pairs, right.shape[0])
    rows_f = one_hot_rows(order % form_count, form.shape[0])
    column = (momenta % LX)[None, :]
    tables = (form, rows_l, rows_r, rows_f)
    bounds = [0, points // 2, points * 3 // 4, points]
    spans = list(zip(bounds[:-1], bounds[1:]))
    parts = [my_window[lo:hi] for lo, hi in spans]
    loops = [loop_matrices(parts[0], column, left, right, *tables)]
    loops, right, below, above = lax.optimization_barrier((loops, right, below, above))
    far_below = [lax.ppermute(piece, "mom", [(1, 2)]) for piece in below]
    far_above = [lax.ppermute(piece, "mom", [(2, 1)]) for piece in above]

    sums, sent = [], []
    for i in range(CHUNKS):
        stack = jnp.concatenate([far_below[i], below[i], pieces[i], above[i], far_above[i]], axis=0)
        tiles = stack.reshape(5 * points, chunk_pairs, form_count, col_count)
        both = jnp.einsum("qplm,pamc->qalc", weights, tiles, preferred_element_type=jnp.float32)
        both = both.reshape(2 * points, chunk_rows, col_count)
        sums.append(both[:points])
        sent.append(both[points:].astype(jnp.bfloat16))
    sent[-1], right = lax.optimization_barrier((sent[-1], right))
    outer = [lax.ppermute(each, "mom", [(2, 3), (1, 0)]) for each in sent]
    loops.append(loop_matrices(parts[1], column, left, right, *tables))

    merged, halves, across, beside = [], [], [], []
    swap = [(0, 1), (1, 0)]
    for i in range(CHUNKS):
        mine = vertex_own[:, i * chunk_rows : (i + 1) * chunk_rows].astype(jnp.float32)
        if i == 0:
            outer[0], loops[1] = lax.optimization_barrier((outer[0], loops[1]))
        mine = (mine + sums[i] + outer[i].astype(jnp.float32)).astype(jnp.bfloat16)
        if i == 0:
            mine, right = lax.optimization_barrier((mine, right))
            loops.append(loop_matrices(parts[2], column, left, right, *tables))
        merged.append(mine)
        across.append(lax.ppermute(mine, "orb", swap))
        beside.append(lax.ppermute(mine, "ff", swap))
    for i in range(CHUNKS):
        rows = jnp.concatenate([merged[i], beside[i]], axis=2)
        terms = [
            jnp.einsum("qrj,qji->qri", rows[lo:hi], loop, preferred_element_type=jnp.float32)
            for (lo, hi), loop in zip(spans, loops)
        ]
        halves.append(jnp.concatenate(terms, axis=0).astype(jnp.bfloat16))
    half = jnp.concatenate(halves, axis=1)
    tall = jnp.concatenate(merged + across, axis=1)
    change = jnp.einsum("qri,qic->qrc", half, tall, preferred_element_type=jnp.float32)
    total = jnp.concatenate(merged, axis=1).astype(jnp.float32) + change
    return total.astype(jnp.bfloat16)


def solution(mesh):
    sizes = dict(mesh.shape)
    in_line = sizes["mom"] == ENDS and sizes["orb"] == 2 and sizes["ff"] == 2
    return jax.shard_map(
        body_line if in_line else body_gathered,
        mesh=mesh,
        in_specs=(
            P(("grp", "mom"), "orb", "ff"),
            P(("grp", "mom"), "orb", "ff"),
            P("mom", None, None, None),
            P("grp", None),
            P("grp", None),
            P(),
            P(),
        ),
        out_specs=P(("grp", "mom"), "orb", "ff"),
        check_vma=False,
    )
```
